256 devices in a mesh: grp: 2 (over x_lo), seq: 64 (over z, y, core), tp: 2 (over x_hi).
Axes of the slice: x: 4 (x_hi: 2, x_lo: 2; x = x_hi * 2 + x_lo), y: 4, z: 8, core: 2. Of those that a mesh axis runs over, the one named last changes fastest.
Arguments:
- queries: bfloat16 [106496, 2048], P('seq', ('grp', 'tp')), may hold values from -6 to 6
- cotangent: bfloat16 [106496, 2048], P('seq', ('grp', 'tp')), may hold values from -48 to 48
- neighbour_keys: bfloat16 [512, 128, 2048], P('seq', None, ('grp', 'tp')), may hold values from -6 to 6
- neighbour_values: bfloat16 [512, 128, 2048], P('seq', None, ('grp', 'tp')), may hold values from -6 to 6
- nbr_owner: int32 [1664, 2], replicated, may hold values from 0 to 63, all different within a row; in each aligned block of 26 rows (0 to 25, 26 to 51, ...) at most 2 rows name the same one
- nbr_slot: int32 [1664, 2], replicated, may hold values from 0 to 7
Outputs:
- attention: bfloat16 [106496, 2048], P('seq', ('grp', 'tp'))
- key_grad: bfloat16 [512, 128, 2048], P('seq', None, ('grp', 'tp'))
- value_grad: bfloat16 [512, 128, 2048], P('seq', None, ('grp', 'tp'))
The draws below stay inside these ranges and needn't reach their ends.
Inputs may be any that keep to these rules, and one draw needn't show every extreme that they name: `nbr_owner`: row b names the owners (indices along seq) of the two neighbours that token block b attends; the two differ. Among the 26 rows of one device no owner is named more than 2 times, and in the rows of some devices one owner is named exactly 2 times.
All inputs are finite; a program needn't handle non-finite values.
Results may differ from the reference program's by a relative error of at most 0.0057.
Values may be sent and summed in bfloat16 or wider, within the bound.
No kernel may reach another device: no remote copies, remote signals or barrier semaphores. Data moves between devices by JAX's collectives and lax.ppermute only.
A program may use at most 192 MiB of HBM per device.

```python
import math
import jax
import jax.numpy as jnp
import numpy as np
from jax import lax

HEADS = 16
HDIM = 128
BLOCK = 64
NLEN = 128
BLOCKS_DEV = 26
NB_DEV = 8
CAP = 2
TOKENS = 106496
NBLOCKS = 1664
NEIGH = 512
N_SEQ = 64


def draw_queries(key, part):
    key = jax.random.fold_in(key, 7)
    key_base = jax.random.fold_in(key, 0)
    entries = jnp.clip(jax.random.normal(key_base, (TOKENS, HEADS, HDIM), jnp.float32), -6.0, 6.0)
    return entries.reshape(TOKENS, HEADS * HDIM).astype(jnp.bfloat16)


def draw_neighbour_keys(key, part):
    key = jax.random.fold_in(key, 13)
    key_base = jax.random.fold_in(key, 0)
    entries = jnp.clip(jax.random.normal(key_base, (NEIGH, NLEN, HEADS, HDIM), jnp.float32), -6.0, 6.0)
    return entries.reshape(NEIGH, NLEN, HEADS * HDIM).astype(jnp.bfloat16)


def with_ends(values, stream_key, low, high):
    index_at = [jax.random.randint(jax.random.fold_in(stream_key, axis), (), 0, length) for axis, length in enumerate(values.shape)]
    widest = values.shape.index(max(values.shape))
    next_to = index_at[:widest] + [(index_at[widest] + 1) % values.shape[widest]] + index_at[widest + 1:]
    return values.at[tuple(index_at)].set(low).at[tuple(next_to)].set(high)


def block_scale(key, extent, cuts, least, top_value):
    loudness, own = 1.0, jax.random.fold_in(key, 6)
    for position, shards_of in cuts:
        heights = jnp.exp(jax.random.uniform(jax.random.fold_in(own, position), (shards_of,), jnp.float32, least / len(cuts), top_value / len(cuts)))
        loudness = loudness * jnp.repeat(heights, extent[position] // shards_of).reshape([-1 if axis == position else 1 for axis in range(len(extent))])
    return loudness


def routed_block(key, own, number, rows, number_of, top, reach, skew):
    order = jax.random.permutation(key, number_of)
    crowded, common = portions_of(number_of, rows * top, reach, skew, True), portions_of(number_of, rows * top, reach, skew, False)
    places = jnp.arange(number_of)

    def named(tallies, rotation):
        used = int((tallies > 0).sum())
        fixed = max(1, used // 4)
        passed = fixed + (places - fixed + rotation * (used - fixed)) % max(1, number_of - fixed)
        return jnp.zeros((number_of,), jnp.int32).at[order[jnp.where(places < fixed, places, passed)]].set(jnp.asarray(tallies, jnp.int32))

    tallies = jnp.where(number % 4 == 0, named(crowded, number // 4), named(common, number - number // 4 - 1))
    mixed = jax.random.permutation(jax.random.fold_in(own, 3), number_of)
    source_of, sink = mixed[0:number_of // 2 * 2:2], mixed[1:number_of // 2 * 2:2]
    margin = jnp.minimum(tallies[source_of] - 1, reach - tallies[sink]) // 2
    margin = jnp.where((source_of == order[0]) | (sink == order[0]) | (tallies[sink] == 0), 0, jnp.maximum(margin, 0))
    passed = jax.random.randint(jax.random.fold_in(own, 4), (number_of // 2,), 0, 1 << 20) % (margin + 1)
    tallies = tallies.at[source_of].add(-passed).at[sink].add(passed)
    members = jnp.searchsorted(jnp.cumsum(tallies), jnp.arange(rows * top), side="right").astype(jnp.int32)
    table = members.reshape(top, rows).T
    table = table[jax.random.permutation(jax.random.fold_in(own, 1), rows)]
    rotation = jax.random.randint(jax.random.fold_in(own, 2), (rows, 1), 0, top)
    return jnp.take_along_axis(table, (jnp.arange(top)[None, :] + rotation) % top, axis=1)


def portions_of(number_of, total, bound, slope, full):
    loads = [(1 << 20) // math.isqrt(rank ** slope) + 1 for rank in range(1, number_of + 1)]
    largest = bound if full else min(bound, max(-(-total // number_of), total * loads[0] // sum(loads)))
    least = 1 if total - largest >= number_of - 1 else 0
    given, surplus = [largest] + [least] * (number_of - 1), total - largest - least * (number_of - 1)
    while surplus > 0:
        free = [i for i in range(1, number_of) if given[i] < largest] or [i for i in range(1, number_of) if given[i] < bound]
        pool, remaining = sum([loads[i] for i in free]), surplus
        for i in free:
            addition = min(bound - given[i], max(1, remaining * loads[i] // pool), surplus)
            given[i] = given[i] + addition
            surplus = surplus - addition
    return np.array(given)


def centred(key, dims, spread, bound, pieces=(), kind=jnp.bfloat16):
    drawn = spread * jax.random.normal(key, dims, jnp.float32)
    if pieces:
        drawn = drawn * block_scale(key, dims, pieces, -0.22, 0.18)
    return jnp.clip(drawn, -bound, bound).astype(kind)


def setup_inputs(seed: int = 0) -> dict:
    streams_of = jax.random.split(jax.random.key(seed), 7)
    queries = draw_queries(jax.random.fold_in(streams_of[6], 71), 0)
    cotangent = centred(streams_of[1], (TOKENS, HEADS * HDIM), 8.0, 48.0, ((0, 64), (1, 4)))
    neighbour_keys = draw_neighbour_keys(jax.random.fold_in(streams_of[6], 71), 0)
    neighbour_values = centred(streams_of[3], (NEIGH, NLEN, HEADS * HDIM), 1.0, 6.0, ((0, 64), (2, 4)))
    nbr_owner_keys = jax.random.split(jax.random.fold_in(streams_of[4], 1), NBLOCKS // BLOCKS_DEV)
    nbr_owner_turns = jax.random.permutation(jax.random.fold_in(streams_of[4], 3), NBLOCKS // BLOCKS_DEV)
    nbr_owner = jax.vmap(lambda own, number: routed_block(jax.random.fold_in(streams_of[4], 2), own, number, BLOCKS_DEV, N_SEQ, 2, CAP, 2))(nbr_owner_keys, nbr_owner_turns).reshape((NBLOCKS, 2))
    nbr_slot = with_ends(jax.random.randint(streams_of[5], (NBLOCKS, 2), 0, NB_DEV), jax.random.fold_in(streams_of[5], 1), 0, NB_DEV - 1).astype(jnp.int32)
    return dict(queries=queries, cotangent=cotangent, neighbour_keys=neighbour_keys, neighbour_values=neighbour_values, nbr_owner=nbr_owner, nbr_slot=nbr_slot)


def rounded(tensor):
    return lax.optimization_barrier(tensor.astype(jnp.bfloat16))

def head_pass(query_head, cot_head, key_head, value_head, pair_ids):
    score_scale = 1.0 / math.sqrt(HDIM)
    flat_ids = pair_ids.reshape(-1)
    near_keys = key_head[pair_ids].astype(jnp.float32)
    near_values = value_head[pair_ids].astype(jnp.float32)
    query_f = query_head.astype(jnp.float32)
    cot_f = cot_head.astype(jnp.float32)
    scores = jnp.einsum('brd,bjkd->bjrk', query_f, near_keys) * score_scale
    local_max = lax.optimization_barrier(jnp.max(scores, axis=-1, keepdims=True))
    part_lse = local_max + jnp.log(lax.optimization_barrier(jnp.sum(jnp.exp(scores - local_max), axis=-1, keepdims=True)))
    local_prob = rounded(jnp.exp(scores - part_lse)).astype(jnp.float32)
    partial_out = rounded(jnp.einsum('bjrk,bjkd->bjrd', local_prob, near_values)).astype(jnp.float32)
    largest = lax.optimization_barrier(jnp.max(part_lse, axis=1, keepdims=True))
    total_lse = largest + jnp.log(lax.optimization_barrier(jnp.sum(jnp.exp(part_lse - largest), axis=1, keepdims=True)))
    shares = jnp.exp(part_lse - total_lse)
    attended = lax.optimization_barrier(jnp.sum(shares * partial_out, axis=1))
    inner_sum = lax.optimization_barrier(jnp.sum(cot_f * attended, axis=-1))
    full_prob = jnp.exp(scores - total_lse)
    prob_low = rounded(full_prob).astype(jnp.float32)
    value_pairs = jnp.einsum('bjrk,brd->bjkd', prob_low, cot_f)
    dot_grad = jnp.einsum('brd,bjkd->bjrk', cot_f, near_values)
    score_grad = rounded(full_prob * (dot_grad - inner_sum[:, None, :, None])).astype(jnp.float32)
    key_pairs = jnp.einsum('bjrk,brd->bjkd', score_grad, query_f) * score_scale
    key_grad = jax.ops.segment_sum(key_pairs.reshape(-1, NLEN, HDIM), flat_ids, NEIGH)
    value_grad = jax.ops.segment_sum(value_pairs.reshape(-1, NLEN, HDIM), flat_ids, NEIGH)
    return (attended, key_grad, value_grad)

def reference(queries, cotangent, neighbour_keys, neighbour_values, nbr_owner, nbr_slot):
    pair_ids = (nbr_owner * NB_DEV + nbr_slot).astype(jnp.int32)
    query_heads = queries.reshape(NBLOCKS, BLOCK, HEADS, HDIM).transpose(2, 0, 1, 3)
    cot_heads = cotangent.reshape(NBLOCKS, BLOCK, HEADS, HDIM).transpose(2, 0, 1, 3)
    key_heads = neighbour_keys.reshape(NEIGH, NLEN, HEADS, HDIM).transpose(2, 0, 1, 3)
    value_heads = neighbour_values.reshape(NEIGH, NLEN, HEADS, HDIM).transpose(2, 0, 1, 3)

    def per_head(operands):
        return head_pass(operands[0], operands[1], operands[2], operands[3], pair_ids)
    attended, key_grad, value_grad = lax.map(per_head, (query_heads, cot_heads, key_heads, value_heads))
    attention = attended.astype(jnp.bfloat16).transpose(1, 2, 0, 3).reshape(TOKENS, HEADS * HDIM)
    key_out = key_grad.transpose(1, 2, 0, 3).reshape(NEIGH, NLEN, HEADS * HDIM).astype(jnp.bfloat16)
    value_out = value_grad.transpose(1, 2, 0, 3).reshape(NEIGH, NLEN, HEADS * HDIM).astype(jnp.bfloat16)
    return (attention, key_out, value_out)
```

```python
import functools
import math

import jax
import jax.numpy as jnp
from jax import lax
from jax.experimental import pallas as pl
from jax.experimental.pallas import tpu as pltpu
from jax.sharding import Mesh, PartitionSpec as P

HDIM = 128
BLOCK = 64
NLEN = 128
ROW = 8
LEVELS = 8
CAPACITY = 2
PAIR_WIDTH = 2 * HDIM
SCALE = 1.0 / math.sqrt(HDIM)
VMEM_LIMIT = 48 * 1024 * 1024
ORDER = (0, 7, 1, 6, 2, 5, 3, 4)
GROUPS = ((0, 1), (1, 2), (3, 2), (5, 2), (7, 1))
LEVEL_SLOTS = ROW * CAPACITY


def lookup(table, index):
    return sum(jnp.where(index == i, jnp.int32(v), 0) for i, v in enumerate(table))


def count(mask, axis):
    return jnp.sum(mask.astype(jnp.int32), axis=axis)


def route(nbr_owner, nbr_slot, z, r, near_dev, blocks_dev):
    row_blocks = ROW * blocks_dev
    owner = lax.dynamic_slice_in_dim(nbr_owner, z * row_blocks, row_blocks).reshape(-1)
    slot = lax.dynamic_slice_in_dim(nbr_slot, z * row_blocks, row_blocks).reshape(-1)
    pairs = owner.shape[0]
    place = jnp.arange(pairs, dtype=jnp.int32)
    block = place // 2
    worker = owner % ROW
    position = lookup([ORDER.index(d) for d in range(LEVELS)], (owner // ROW - z) % LEVELS)
    group = lookup([g for g, (_, size) in enumerate(GROUPS) for _ in range(size)], position)
    first_slot = lookup([first * LEVEL_SLOTS for first, _ in GROUPS], group)
    near = position * near_dev + slot
    order = near * pairs + place
    same_worker = worker[None, :] == worker[:, None]
    ahead = (order[None, :] < order[:, None]) & same_worker & (group[None, :] == group[:, None])
    work_slot = first_slot + count(ahead, 1)
    slots = LEVELS * LEVEL_SLOTS
    other_slot = (worker * slots + work_slot).reshape(-1, 2)[:, ::-1].reshape(-1)
    home = block // blocks_dev
    earlier = (place[None, :] < place[:, None]) & same_worker & (home[None, :] == home[:, None])
    home_rank = count(earlier, 1)
    out_slot = home * LEVEL_SLOTS + home_rank
    back_slot = lax.dynamic_slice_in_dim(
        worker * LEVEL_SLOTS + home_rank, r * 2 * blocks_dev, 2 * blocks_dev
    )
    mine = worker == r
    hit = mine[None, :] & (work_slot[None, :] == jnp.arange(slots, dtype=jnp.int32)[:, None])

    def listed(values):
        return jnp.sum(jnp.where(hit, values[None, :], 0), axis=1)

    rows = jnp.arange(LEVELS * near_dev, dtype=jnp.int32)
    in_group = mine[None, :] & (
        group[None, :]
        == lookup([g for g, (_, size) in enumerate(GROUPS) for _ in range(size)], rows // near_dev)[:, None]
    )
    row_first = lookup(
        [first * LEVEL_SLOTS for first, size in GROUPS for _ in range(size)], rows // near_dev
    )
    low = row_first + count(in_group & (near[None, :] < rows[:, None]), 1)
    high = row_first + count(in_group & (near[None, :] <= rows[:, None]), 1)
    own = r * slots + jnp.arange(slots, dtype=jnp.int32)
    return low, high, listed(block), jnp.stack([own, listed(other_slot)]), listed(out_slot), back_slot


def two_heads(x):
    gap = jnp.zeros((BLOCK, HDIM), x.dtype)
    first = jnp.concatenate([x[:, :HDIM], gap], axis=1)
    second = jnp.concatenate([gap, x[:, HDIM:]], axis=1)
    return jnp.concatenate([first, second], axis=0)


def product(a, b, dims):
    return lax.dot_general(a, b, (dims, ((), ())), preferred_element_type=jnp.float32)


def fetch(source, buffer, sems, block, j):
    return pltpu.make_async_copy(source.at[block], buffer.at[j], sems.at[j])


def walk(first_slot, first_row, sizes, low, high, block_of, sources, step):
    rows = sum(sizes)

    def start(i, carry):
        for source, buffer, sems in sources:
            fetch(source, buffer, sems, block_of[i], i - first_slot).start()
        return carry

    lax.fori_loop(low[first_row], high[first_row + rows - 1], start, 0)
    done = 0
    for a, size in enumerate(sizes):
        offset = first_row + done

        def near(m, carry, a=a, offset=offset):
            step(a, m, low[offset + m], high[offset + m])
            return carry

        lax.fori_loop(0, size, near, 0)
        done += size


def arrive(sources, block, j):
    for source, buffer, sems in sources:
        fetch(source, buffer, sems, block, j).wait()


def stat_kernel(first_slot, first_row, sizes, low, high, block_of, q_hbm, c_hbm, *refs):
    near_refs = refs[: 2 * len(sizes)]
    stat_ref, q_buf, c_buf, q_sem, c_sem = refs[2 * len(sizes) :]
    sources = ((q_hbm, q_buf, q_sem), (c_hbm, c_buf, c_sem))
    width = q_buf.shape[2]

    def near(a, m, begin, end):
        k_ref, v_ref = near_refs[2 * a], near_refs[2 * a + 1]

        def pair(i, carry):
            j = i - first_slot
            arrive(sources, block_of[i], j)
            rows = []
            for g in range(width // PAIR_WIDTH):
                cols = slice(g * PAIR_WIDTH, (g + 1) * PAIR_WIDTH)
                scores = product(k_ref[m, :, cols], two_heads(q_buf[j, :, cols]), ((1,), (1,))) * SCALE
                dots = product(v_ref[m, :, cols], two_heads(c_buf[j, :, cols]), ((1,), (1,)))
                top = jnp.max(scores, axis=0, keepdims=True)
                weights = jnp.exp(scores - top)
                total = jnp.sum(weights, axis=0, keepdims=True)
                rows.append(top + jnp.log(total))
                rows.append(jnp.sum(weights * dots, axis=0, keepdims=True) / total)
            stat_ref[j] = jnp.concatenate(rows, axis=0)
            return carry

        lax.fori_loop(begin, end, pair, 0)

    walk(first_slot, first_row, sizes, low, high, block_of, sources, near)


def grad_kernel(
    first_slot, first_row, sizes, ahead, low, high, block_of, stat_of, out_slot, q_hbm, c_hbm, stat_ref, *refs
):
    refs = refs[ahead:]
    near_refs = refs[: 2 * len(sizes)]
    o_hbm = refs[2 * len(sizes)]
    grad_refs = refs[2 * len(sizes) + 1 : 4 * len(sizes) + 1]
    q_buf, c_buf, o_buf, q_sem, c_sem, o_sem = refs[4 * len(sizes) + 1 :]
    sources = ((q_hbm, q_buf, q_sem), (c_hbm, c_buf, c_sem))
    width = q_buf.shape[2]

    def near(a, m, begin, end):
        k_ref, v_ref = near_refs[2 * a], near_refs[2 * a + 1]
        dk_ref, dv_ref = grad_refs[2 * a], grad_refs[2 * a + 1]
        dk_ref[m] = jnp.zeros(dk_ref.shape[1:], dk_ref.dtype)
        dv_ref[m] = jnp.zeros(dv_ref.shape[1:], dv_ref.dtype)

        def pair(i, carry):
            j = i - first_slot
            own = stat_ref[stat_of[0, i]]
            other = stat_ref[stat_of[1, i]]
            arrive(sources, block_of[i], j)
            results = []
            for g in range(width // PAIR_WIDTH):
                cols = slice(g * PAIR_WIDTH, (g + 1) * PAIR_WIDTH)
                lse, other_lse = own[2 * g : 2 * g + 1], other[2 * g : 2 * g + 1]
                top = jnp.maximum(lse, other_lse)
                total = top + jnp.log(jnp.exp(lse - top) + jnp.exp(other_lse - top))
                inner = (
                    jnp.exp(lse - total) * own[2 * g + 1 : 2 * g + 2]
                    + jnp.exp(other_lse - total) * other[2 * g + 1 : 2 * g + 2]
                )
                keys, values = k_ref[m, :, cols], v_ref[m, :, cols]
                query, cot = two_heads(q_buf[j, :, cols]), two_heads(c_buf[j, :, cols])
                prob = jnp.exp(product(keys, query, ((1,), (1,))) * SCALE - total)
                dots = product(values, cot, ((1,), (1,)))
                score_grad = (prob * (dots - inner)).astype(jnp.bfloat16)
                prob = prob.astype(jnp.bfloat16)
                both = product(prob, values, ((0,), (0,)))
                results.append(
                    (
                        cols,
                        product(score_grad, query, ((1,), (0,))),
                        product(prob, cot, ((1,), (0,))),
                        jnp.concatenate([both[:BLOCK, :HDIM], both[BLOCK:, HDIM:]], axis=1),
                    )
                )
            for cols, dk, dv, out in results:
                dk_ref[m, :, cols] += dk
                dv_ref[m, :, cols] += dv
                o_buf[j, :, cols] = out.astype(o_buf.dtype)
            pltpu.make_async_copy(o_buf.at[j], o_hbm.at[out_slot[i]], o_sem.at[j]).start()
            return carry

        lax.fori_loop(begin, end, pair, 0)

    walk(first_slot, first_row, sizes, low, high, block_of, sources, near)

    def finish(i, carry):
        j = i - first_slot
        pltpu.make_async_copy(o_buf.at[j], o_hbm.at[out_slot[i]], o_sem.at[j]).wait()
        return carry

    lax.fori_loop(low[first_row], high[first_row + sum(sizes) - 1], finish, 0)


def join_kernel(slot_of, parts_hbm, out_ref, buffer, sems):
    blocks = out_ref.shape[0]

    def start(i, carry):
        fetch(parts_hbm, buffer, sems, slot_of[i], i).start()
        return carry

    def join(b, carry):
        for i in (2 * b, 2 * b + 1):
            fetch(parts_hbm, buffer, sems, slot_of[i], i).wait()
        parts = [buffer[i].astype(jnp.float32) for i in (2 * b, 2 * b + 1)]
        out_ref[b] = (parts[0] + parts[1]).astype(out_ref.dtype)
        return carry

    lax.fori_loop(0, 2 * blocks, start, 0)
    lax.fori_loop(0, blocks, join, 0)


SMEM = pl.BlockSpec(memory_space=pltpu.SMEM)
VMEM = pl.BlockSpec(memory_space=pltpu.VMEM)
HBM = pl.BlockSpec(memory_space=pl.ANY)
PARAMS = pltpu.CompilerParams(vmem_limit_bytes=VMEM_LIMIT)


def body(queries, cotangent, neighbour_keys, neighbour_values, nbr_owner, nbr_slot):
    z = lax.axis_index("z")
    r = lax.axis_index("row")
    token_rows, width = queries.shape
    blocks_dev = token_rows // BLOCK
    row_blocks = ROW * blocks_dev
    near_dev = neighbour_keys.shape[0]
    half = near_dev // 2
    slots = LEVELS * LEVEL_SLOTS
    stat_rows = 2 * (width // PAIR_WIDTH)
    up = [(i, (i + 1) % LEVELS) for i in range(LEVELS)]
    down = [(i, (i - 1) % LEVELS) for i in range(LEVELS)]

    def move(x, way):
        return lax.ppermute(x, "z", way)

    own = (neighbour_keys, neighbour_values)
    near = [[own]]
    upward, downward = own, own
    for step in range(1, 4):
        upward = tuple(move(x, up) for x in upward)
        downward = tuple(move(x, down) for x in downward)
        near.append([upward, downward])
    near.append(
        [
            tuple(move(x[:half], up) for x in upward),
            tuple(move(x[half:], down) for x in downward),
        ]
    )

    row_queries = lax.all_gather(queries, "row", axis=0, tiled=True).reshape(row_blocks, BLOCK, width)
    row_cot = lax.all_gather(cotangent, "row", axis=0, tiled=True).reshape(row_blocks, BLOCK, width)
    low, high, block_of, stat_of, out_slot, back_slot = route(
        nbr_owner, nbr_slot, z, r, near_dev, blocks_dev
    )

    def layout(g):
        position, distances = GROUPS[g]
        arrays = [x for pair in near[g] for x in pair]
        sizes = tuple(pair[0].shape[0] for pair in near[g])
        room = distances * LEVEL_SLOTS
        buffers = [pltpu.VMEM((room, BLOCK, width), jnp.bfloat16)] * 2
        sems = [pltpu.SemaphoreType.DMA((room,))] * 2
        return position * LEVEL_SLOTS, position * near_dev, sizes, arrays, room, buffers, sems

    stats = []
    for g in range(len(GROUPS)):
        first_slot, first_row, sizes, arrays, room, buffers, sems = layout(g)
        stats.append(
            pl.pallas_call(
                functools.partial(stat_kernel, first_slot, first_row, sizes),
                in_specs=[SMEM] * 3 + [HBM] * 2 + [VMEM] * len(arrays),
                out_specs=VMEM,
                out_shape=jax.ShapeDtypeStruct((room, stat_rows, NLEN), jnp.float32),
                scratch_shapes=buffers + sems,
                compiler_params=PARAMS,
                cost_estimate=pl.CostEstimate(
                    flops=room * 10**7, bytes_accessed=room * 10**6, transcendentals=room * 10**4
                ),
            )(low, high, block_of, row_queries, row_cot, *arrays)
        )
    row_stats = lax.all_gather(jnp.concatenate(stats, axis=0), "row", axis=0, tiled=True)

    out = jax.ShapeDtypeStruct((slots, BLOCK, width), jnp.bfloat16)

    def gradients(g, out, after):
        first_slot, first_row, sizes, arrays, room, buffers, sems = layout(g)
        ahead = list(after) if isinstance(out, jax.ShapeDtypeStruct) else [*after, out]
        results = pl.pallas_call(
            functools.partial(grad_kernel, first_slot, first_row, sizes, len(ahead)),
            in_specs=[SMEM] * 5 + [HBM] * 2 + [VMEM] + [HBM] * len(ahead) + [VMEM] * len(arrays),
            out_specs=[HBM] + [VMEM] * len(arrays),
            out_shape=[jax.ShapeDtypeStruct(out.shape, out.dtype)]
            + [jax.ShapeDtypeStruct(x.shape, jnp.float32) for x in arrays],
            scratch_shapes=buffers + buffers[:1] + sems + sems[:1],
            input_output_aliases={7 + len(ahead): 0} if len(ahead) > len(after) else {},
            compiler_params=PARAMS,
            cost_estimate=pl.CostEstimate(
                flops=room * 10**7, bytes_accessed=room * 17 * 10**5, transcendentals=room * 10**4
            ),
        )(low, high, block_of, stat_of, out_slot, row_queries, row_cot, row_stats, *ahead, *arrays)
        return results[0], [(results[1 + 2 * a] * SCALE, results[2 + 2 * a]) for a in range(len(sizes))]

    def narrow(x):
        return x.astype(jnp.bfloat16)

    def wide(x):
        return x.astype(jnp.float32)

    out, grads = gradients(4, out, ())
    downward = tuple(move(narrow(x), down) for x in grads[0])
    upward = tuple(move(narrow(x), up) for x in grads[1])
    out, grads = gradients(3, out, ())
    downward = tuple(
        narrow(jnp.concatenate([wide(a) + b[:half], b[half:]], axis=0)) for a, b in zip(downward, grads[0])
    )
    upward = tuple(
        narrow(jnp.concatenate([b[:half], wide(a) + b[half:]], axis=0)) for a, b in zip(upward, grads[1])
    )
    out, far = gradients(2, out, (*downward, *upward))
    out, middle = gradients(1, out, ())
    downward = tuple(move(x, down) for x in downward)
    upward = tuple(move(x, up) for x in upward)
    out, close = gradients(0, out, (*downward, *upward))
    for grads in (far, middle):
        downward = tuple(move(narrow(wide(a) + b), down) for a, b in zip(downward, grads[0]))
        upward = tuple(move(narrow(wide(a) + b), up) for a, b in zip(upward, grads[1]))
    key_grad, value_grad = (
        narrow(wide(a) + wide(b) + c) for a, b, c in zip(downward, upward, close[0])
    )

    returned = lax.all_to_all(out, "row", split_axis=0, concat_axis=0, tiled=True)
    attention = pl.pallas_call(
        join_kernel,
        in_specs=[SMEM, HBM],
        out_specs=VMEM,
        out_shape=jax.ShapeDtypeStruct((blocks_dev, BLOCK, width), jnp.bfloat16),
        scratch_shapes=[
            pltpu.VMEM((2 * blocks_dev, BLOCK, width), jnp.bfloat16),
            pltpu.SemaphoreType.DMA((2 * blocks_dev,)),
        ],
        compiler_params=PARAMS,
        cost_estimate=pl.CostEstimate(flops=10**7, bytes_accessed=2 * 10**7, transcendentals=0),
    )(back_slot, returned)
    return attention.reshape(token_rows, width), key_grad, value_grad


def solution(mesh):
    grp, seq, tp = (mesh.shape[name] for name in ("grp", "seq", "tp"))
    fine = Mesh(mesh.devices.reshape(grp, seq // ROW, ROW, tp), ("grp", "z", "row", "tp"))
    rows, heads = ("z", "row"), ("grp", "tp")
    return jax.shard_map(
        body,
        mesh=fine,
        in_specs=(
            P(rows, heads),
            P(rows, heads),
            P(rows, None, heads),
            P(rows, None, heads),
            P(),
            P(),
        ),
        out_specs=(P(rows, heads), P(rows, None, heads), P(rows, None, heads)),
        check_vma=False,
    )
```

```python
import functools
import math

import jax
import jax.numpy as jnp
from jax import lax
from jax.experimental import pallas as pl
from jax.experimental.pallas import tpu as pltpu
from jax.sharding import Mesh, PartitionSpec as P

HDIM = 128
BLOCK = 64
NLEN = 128
ROW = 8
LEVELS = 8
CAPACITY = 2
PAIR_WIDTH = 2 * HDIM
SCALE = 1.0 / math.sqrt(HDIM)
VMEM_LIMIT = 48 * 1024 * 1024
ORDER = (0, 7, 1, 6, 2, 5, 3, 4)
GROUPS = ((0, 1), (1, 2), (3, 2), (5, 2), (7, 1))
KEEP_DEPTH = 16
LEVEL_SLOTS = ROW * CAPACITY


def lookup(table, index):
    return sum(jnp.where(index == i, jnp.int32(v), 0) for i, v in enumerate(table))


def count(mask, axis):
    return jnp.sum(mask.astype(jnp.int32), axis=axis)


def route(nbr_owner, nbr_slot, z, r, near_dev, blocks_dev):
    row_blocks = ROW * blocks_dev
    owner = lax.dynamic_slice_in_dim(nbr_owner, z * row_blocks, row_blocks).reshape(-1)
    slot = lax.dynamic_slice_in_dim(nbr_slot, z * row_blocks, row_blocks).reshape(-1)
    pairs = owner.shape[0]
    place = jnp.arange(pairs, dtype=jnp.int32)
    block = place // 2
    worker = owner % ROW
    position = lookup([ORDER.index(d) for d in range(LEVELS)], (owner // ROW - z) % LEVELS)
    group = lookup([g for g, (_, size) in enumerate(GROUPS) for _ in range(size)], position)
    first_slot = lookup([first * LEVEL_SLOTS for first, _ in GROUPS], group)
    near = position * near_dev + slot
    order = near * pairs + place
    same_worker = worker[None, :] == worker[:, None]
    ahead = (order[None, :] < order[:, None]) & same_worker & (group[None, :] == group[:, None])
    work_slot = first_slot + count(ahead, 1)
    slots = LEVELS * LEVEL_SLOTS
    other_slot = (worker * slots + work_slot).reshape(-1, 2)[:, ::-1].reshape(-1)
    home = block // blocks_dev
    earlier = (place[None, :] < place[:, None]) & same_worker & (home[None, :] == home[:, None])
    home_rank = count(earlier, 1)
    out_slot = home * LEVEL_SLOTS + home_rank
    back_slot = lax.dynamic_slice_in_dim(
        worker * LEVEL_SLOTS + home_rank, r * 2 * blocks_dev, 2 * blocks_dev
    )
    mine = worker == r
    hit = mine[None, :] & (work_slot[None, :] == jnp.arange(slots, dtype=jnp.int32)[:, None])

    def listed(values):
        return jnp.sum(jnp.where(hit, values[None, :], 0), axis=1)

    rows = jnp.arange(LEVELS * near_dev, dtype=jnp.int32)
    in_group = mine[None, :] & (
        group[None, :]
        == lookup([g for g, (_, size) in enumerate(GROUPS) for _ in range(size)], rows // near_dev)[:, None]
    )
    row_first = lookup(
        [first * LEVEL_SLOTS for first, size in GROUPS for _ in range(size)], rows // near_dev
    )
    low = row_first + count(in_group & (near[None, :] < rows[:, None]), 1)
    high = row_first + count(in_group & (near[None, :] <= rows[:, None]), 1)
    return low, high, listed(block), listed(other_slot), listed(out_slot), back_slot


def two_heads(x):
    gap = jnp.zeros((BLOCK, HDIM), x.dtype)
    first = jnp.concatenate([x[:, :HDIM], gap], axis=1)
    second = jnp.concatenate([gap, x[:, HDIM:]], axis=1)
    return jnp.concatenate([first, second], axis=0)


def product(a, b, dims):
    return lax.dot_general(a, b, (dims, ((), ())), preferred_element_type=jnp.float32)


def fetch(source, i, j):
    array, buffer, sems, place = source
    return pltpu.make_async_copy(array.at[place(i, j)], buffer.at[j], sems.at[j])


def walk(first_slot, first_row, sizes, low, high, sources, step):
    rows = sum(sizes)

    def start(i, carry):
        for source in sources:
            fetch(source, i, i - first_slot).start()
        return carry

    lax.fori_loop(low[first_row], high[first_row + rows - 1], start, 0)
    done = 0
    for a, size in enumerate(sizes):
        offset = first_row + done

        def near(m, carry, a=a, offset=offset):
            step(a, m, low[offset + m], high[offset + m])
            return carry

        lax.fori_loop(0, size, near, 0)
        done += size


def arrive(sources, i, j):
    for source in sources:
        fetch(source, i, j).wait()


def wait_all(first_slot, first_row, sizes, low, high, copy):
    def finish(i, carry):
        copy(i, i - first_slot).wait()
        return carry

    lax.fori_loop(low[first_row], high[first_row + sum(sizes) - 1], finish, 0)


def stat_kernel(first_slot, first_row, sizes, low, high, block_of, q_hbm, c_hbm, *refs):
    near_hbm = refs[: 2 * len(sizes)]
    stat_ref, kept_hbm, k_buf, v_buf, q_buf, c_buf, kept_buf, k_sem, v_sem, q_sem, c_sem, kept_sem = refs[
        2 * len(sizes) :
    ]
    sources = (
        (q_hbm, q_buf, q_sem, lambda i, j: block_of[i]),
        (c_hbm, c_buf, c_sem, lambda i, j: block_of[i]),
    )
    width = q_buf.shape[2]
    depth = kept_buf.shape[0]
    firsts = [sum(sizes[:a]) for a in range(len(sizes))]

    def bring(a):
        place = pl.ds(firsts[a], sizes[a])
        return (
            pltpu.make_async_copy(near_hbm[2 * a], k_buf.at[place], k_sem.at[a]),
            pltpu.make_async_copy(near_hbm[2 * a + 1], v_buf.at[place], v_sem.at[a]),
        )

    def keep(i, place):
        return pltpu.make_async_copy(kept_buf.at[place], kept_hbm.at[i], kept_sem.at[place])

    def start(i, carry):
        for source in sources:
            fetch(source, i, i - first_slot).start()
        return carry

    def pair(i, n, done):
        j = i - first_slot
        place = done % depth

        @pl.when(done >= depth)
        def _():
            keep(j, place).wait()

        arrive(sources, i, j)
        rows = []
        for g in range(width // PAIR_WIDTH):
            cols = slice(g * PAIR_WIDTH, (g + 1) * PAIR_WIDTH)
            scores = product(k_buf[n, :, cols], two_heads(q_buf[j, :, cols]), ((1,), (1,))) * SCALE
            dots = product(v_buf[n, :, cols], two_heads(c_buf[j, :, cols]), ((1,), (1,)))
            kept_buf[place, :, 2 * g * NLEN : (2 * g + 1) * NLEN] = scores
            kept_buf[place, :, (2 * g + 1) * NLEN : (2 * g + 2) * NLEN] = dots
            top = jnp.max(scores, axis=0, keepdims=True)
            weights = jnp.exp(scores - top)
            total = jnp.sum(weights, axis=0, keepdims=True)
            rows.append(top + jnp.log(total))
            rows.append(jnp.sum(weights * dots, axis=0, keepdims=True) / total)
        stat_ref[j] = jnp.concatenate(rows, axis=0)
        keep(j, place).start()
        return done + 1

    for a in range(len(sizes)):
        for copy in bring(a):
            copy.start()
        begin = first_row + firsts[a]
        lax.fori_loop(low[begin], high[begin + sizes[a] - 1], start, 0)
    done = jnp.int32(0)
    for a in range(len(sizes)):
        for copy in bring(a):
            copy.wait()

        def near(n, done):
            row = first_row + n
            return lax.fori_loop(low[row], high[row], lambda i, done: pair(i, n, done), done)

        done = lax.fori_loop(firsts[a], firsts[a] + sizes[a], near, done)

    def finish(place, carry):
        keep(0, place).wait()
        return carry

    lax.fori_loop(0, jnp.minimum(done, depth), finish, 0)


def grad_kernel(
    first_slot, kept_slot, first_row, sizes, ahead, low, high, block_of, other_of, out_slot,
    q_hbm, c_hbm, kept_hbm, others_hbm, stat_ref, *refs
):
    refs = refs[ahead:]
    value_refs = refs[: len(sizes)]
    o_hbm = refs[len(sizes)]
    grad_refs = refs[len(sizes) + 1 : 3 * len(sizes) + 1]
    q_buf, c_buf, kept_buf, other_buf, o_buf, q_sem, c_sem, kept_sem, other_sem, o_sem = refs[3 * len(sizes) + 1 :]
    sources = (
        (kept_hbm, kept_buf, kept_sem, lambda i, j: i - kept_slot),
        (others_hbm, other_buf, other_sem, lambda i, j: other_of[i]),
        (q_hbm, q_buf, q_sem, lambda i, j: block_of[i]),
        (c_hbm, c_buf, c_sem, lambda i, j: block_of[i]),
    )
    width = q_buf.shape[2]

    def put(i, j):
        return pltpu.make_async_copy(o_buf.at[j], o_hbm.at[out_slot[i]], o_sem.at[j])

    def near(a, m, begin, end):
        v_ref = value_refs[a]
        dk_ref, dv_ref = grad_refs[2 * a], grad_refs[2 * a + 1]
        dk_ref[m] = jnp.zeros(dk_ref.shape[1:], dk_ref.dtype)
        dv_ref[m] = jnp.zeros(dv_ref.shape[1:], dv_ref.dtype)

        def pair(i, carry):
            j = i - first_slot
            arrive(sources, i, j)
            own, other = stat_ref[i - kept_slot], other_buf[j]
            results = []
            for g in range(width // PAIR_WIDTH):
                cols = slice(g * PAIR_WIDTH, (g + 1) * PAIR_WIDTH)
                lse, other_lse = own[2 * g : 2 * g + 1], other[2 * g : 2 * g + 1]
                top = jnp.maximum(lse, other_lse)
                total = top + jnp.log(jnp.exp(lse - top) + jnp.exp(other_lse - top))
                inner = (
                    jnp.exp(lse - total) * own[2 * g + 1 : 2 * g + 2]
                    + jnp.exp(other_lse - total) * other[2 * g + 1 : 2 * g + 2]
                )
                query, cot = two_heads(q_buf[j, :, cols]), two_heads(c_buf[j, :, cols])
                prob = jnp.exp(kept_buf[j, :, 2 * g * NLEN : (2 * g + 1) * NLEN] - total)
                dots = kept_buf[j, :, (2 * g + 1) * NLEN : (2 * g + 2) * NLEN]
                score_grad = (prob * (dots - inner)).astype(jnp.bfloat16)
                prob = prob.astype(jnp.bfloat16)
                both = product(prob, v_ref[m, :, cols], ((0,), (0,)))
                results.append(
                    (
                        cols,
                        product(score_grad, query, ((1,), (0,))) * SCALE,
                        product(prob, cot, ((1,), (0,))),
                        jnp.concatenate([both[:BLOCK, :HDIM], both[BLOCK:, HDIM:]], axis=1),
                    )
                )
            for cols, dk, dv, out in results:
                dk_ref[m, :, cols] += dk
                dv_ref[m, :, cols] += dv
                o_buf[j, :, cols] = out.astype(o_buf.dtype)
            put(i, j).start()
            return carry

        lax.fori_loop(begin, end, pair, 0)

    walk(first_slot, first_row, sizes, low, high, sources, near)
    wait_all(first_slot, first_row, sizes, low, high, put)


def join_kernel(slot_of, parts_hbm, out_ref, buffer, sems):
    blocks = out_ref.shape[0]
    source = (parts_hbm, buffer, sems, lambda i, j: slot_of[i])

    def start(i, carry):
        fetch(source, i, i).start()
        return carry

    def join(b, carry):
        for i in (2 * b, 2 * b + 1):
            fetch(source, i, i).wait()
        parts = [buffer[i].astype(jnp.float32) for i in (2 * b, 2 * b + 1)]
        out_ref[b] = (parts[0] + parts[1]).astype(out_ref.dtype)
        return carry

    lax.fori_loop(0, 2 * blocks, start, 0)
    lax.fori_loop(0, blocks, join, 0)


SMEM = pl.BlockSpec(memory_space=pltpu.SMEM)
VMEM = pl.BlockSpec(memory_space=pltpu.VMEM)
HBM = pl.BlockSpec(memory_space=pl.ANY)
PARAMS = pltpu.CompilerParams(vmem_limit_bytes=VMEM_LIMIT)


def body(queries, cotangent, neighbour_keys, neighbour_values, nbr_owner, nbr_slot):
    z = lax.axis_index("z")
    r = lax.axis_index("row")
    token_rows, width = queries.shape
    blocks_dev = token_rows // BLOCK
    row_blocks = ROW * blocks_dev
    near_dev = neighbour_keys.shape[0]
    half = near_dev // 2
    slots = LEVELS * LEVEL_SLOTS
    stat_rows = 2 * (width // PAIR_WIDTH)
    kept_width = stat_rows * NLEN
    up = [(i, (i + 1) % LEVELS) for i in range(LEVELS)]
    down = [(i, (i - 1) % LEVELS) for i in range(LEVELS)]

    def move(x, way):
        return lax.ppermute(x, "z", way)

    own = (neighbour_keys, neighbour_values)
    near = [[own]]
    upward, downward = own, own
    for step in range(1, 4):
        upward = tuple(move(x, up) for x in upward)
        downward = tuple(move(x, down) for x in downward)
        near.append([upward, downward])
    near.append(
        [
            tuple(move(x[:half], up) for x in upward),
            tuple(move(x[half:], down) for x in downward),
        ]
    )

    row_queries = lax.all_gather(queries, "row", axis=0, tiled=True).reshape(row_blocks, BLOCK, width)
    row_cot = lax.all_gather(cotangent, "row", axis=0, tiled=True).reshape(row_blocks, BLOCK, width)
    low, high, block_of, other_of, out_slot, back_slot = route(
        nbr_owner, nbr_slot, z, r, near_dev, blocks_dev
    )

    def layout(g):
        position, distances = GROUPS[g]
        arrays = [x for pair in near[g] for x in pair]
        sizes = tuple(pair[0].shape[0] for pair in near[g])
        room = distances * LEVEL_SLOTS
        buffers = [pltpu.VMEM((room, BLOCK, width), jnp.bfloat16)] * 2
        buffers.append(pltpu.VMEM((room, NLEN, kept_width), jnp.float32))
        return position * LEVEL_SLOTS, position * near_dev, sizes, arrays, room, buffers

    def behind(x, *others):
        return lax.optimization_barrier((x, *others))[0]

    def statistics(groups):
        near_arrays = [pair for g in groups for pair in near[g]]
        position = GROUPS[groups[0]][0]
        levels = sum(GROUPS[g][1] for g in groups)
        room = levels * LEVEL_SLOTS
        sizes = tuple(pair[0].shape[0] for pair in near_arrays)
        return pl.pallas_call(
            functools.partial(stat_kernel, position * LEVEL_SLOTS, position * near_dev, sizes),
            in_specs=[SMEM] * 3 + [HBM] * (2 + 2 * len(near_arrays)),
            out_specs=[VMEM, HBM],
            out_shape=[
                jax.ShapeDtypeStruct((room, stat_rows, NLEN), jnp.float32),
                jax.ShapeDtypeStruct((room, NLEN, kept_width), jnp.float32),
            ],
            scratch_shapes=[pltpu.VMEM((levels * near_dev, NLEN, width), jnp.bfloat16)] * 2
            + [pltpu.VMEM((room, BLOCK, width), jnp.bfloat16)] * 2
            + [pltpu.VMEM((KEEP_DEPTH, NLEN, kept_width), jnp.float32)]
            + [pltpu.SemaphoreType.DMA((len(near_arrays),))] * 2
            + [pltpu.SemaphoreType.DMA((room,))] * 2
            + [pltpu.SemaphoreType.DMA((KEEP_DEPTH,))],
            compiler_params=PARAMS,
            cost_estimate=pl.CostEstimate(
                flops=10**8, bytes_accessed=levels * 8 * 10**6, transcendentals=10**6
            ),
        )(low, high, block_of, row_queries, row_cot, *[x for pair in near_arrays for x in pair])

    parts = [(0, statistics((0, 1, 2, 3))), (GROUPS[4][0] * LEVEL_SLOTS, statistics((4,)))]
    own_stats = jnp.concatenate([stats for _, (stats, _) in parts], axis=0)
    others = lax.all_gather(own_stats, "row", axis=0, tiled=True)

    def gradients(g, out, after):
        first_slot, first_row, sizes, arrays, room, buffers = layout(g)
        ahead = list(after) if out is None else [*after, out]
        values = arrays[1::2]
        kept_slot, (stats, kept) = parts[g // 4]
        results = pl.pallas_call(
            functools.partial(grad_kernel, first_slot, kept_slot, first_row, sizes, len(ahead)),
            in_specs=[SMEM] * 5 + [HBM] * 4 + [VMEM] + [HBM] * len(ahead) + [VMEM] * len(values),
            out_specs=[HBM] + [VMEM] * len(arrays),
            out_shape=[jax.ShapeDtypeStruct((slots, BLOCK, width), jnp.bfloat16)]
            + [jax.ShapeDtypeStruct(x.shape, jnp.float32) for x in arrays],
            scratch_shapes=buffers
            + [pltpu.VMEM((room, stat_rows, NLEN), jnp.float32), buffers[0]]
            + [pltpu.SemaphoreType.DMA((room,))] * 5,
            input_output_aliases={} if out is None else {9 + len(ahead): 0},
            compiler_params=PARAMS,
            cost_estimate=pl.CostEstimate(
                flops=room * 10**6, bytes_accessed=room * 12 * 10**5, transcendentals=room * 10**4
            ),
        )(low, high, block_of, other_of, out_slot, row_queries, row_cot, kept, others, stats, *ahead, *values)
        return results[0], [(results[1 + 2 * a], results[2 + 2 * a]) for a in range(len(sizes))]

    def narrow(x):
        return x.astype(jnp.bfloat16)

    def wide(x):
        return x.astype(jnp.float32)

    out, grads = gradients(4, None, ())
    downward = tuple(move(narrow(x), down) for x in grads[0])
    upward = tuple(move(narrow(x), up) for x in grads[1])
    out, grads = gradients(3, out, ())
    ends = ((0, half), (0, 0), (0, 0)), ((half, 0), (0, 0), (0, 0))
    downward = tuple(narrow(jnp.pad(wide(a), ends[0]) + b) for a, b in zip(downward, grads[0]))
    upward = tuple(narrow(jnp.pad(wide(a), ends[1]) + b) for a, b in zip(upward, grads[1]))
    out, far = gradients(2, out, (*downward, *upward))
    out, middle = gradients(1, out, ())
    downward = tuple(move(x, down) for x in downward)
    upward = tuple(move(x, up) for x in upward)
    out, close = gradients(0, out, ())
    out = behind(out, *downward, *upward)
    moved = lax.optimization_barrier((*downward, *upward, *close[0]))
    downward, upward = moved[:2], moved[2:4]
    for grads in (far, middle):
        downward = tuple(move(narrow(wide(a) + b), down) for a, b in zip(downward, grads[0]))
        upward = tuple(move(narrow(wide(a) + b), up) for a, b in zip(upward, grads[1]))
    returned = lax.all_to_all(out, "row", split_axis=0, concat_axis=0, tiled=True)
    attention = pl.pallas_call(
        join_kernel,
        in_specs=[SMEM, HBM],
        out_specs=VMEM,
        out_shape=jax.ShapeDtypeStruct((blocks_dev, BLOCK, width), jnp.bfloat16),
        scratch_shapes=[
            pltpu.VMEM((2 * blocks_dev, BLOCK, width), jnp.bfloat16),
            pltpu.SemaphoreType.DMA((2 * blocks_dev,)),
        ],
        compiler_params=PARAMS,
        cost_estimate=pl.CostEstimate(flops=10**7, bytes_accessed=2 * 10**7, transcendentals=0),
    )(back_slot, returned)
    downward = (downward[0], behind(downward[1], attention))
    key_grad, value_grad = (
        narrow(wide(a) + wide(b) + c) for a, b, c in zip(downward, upward, close[0])
    )
    return attention.reshape(token_rows, width), key_grad, value_grad


def solution(mesh):
    grp, seq, tp = (mesh.shape[name] for name in ("grp", "seq", "tp"))
    fine = Mesh(mesh.devices.reshape(grp, seq // ROW, ROW, tp), ("grp", "z", "row", "tp"))
    rows, heads = ("z", "row"), ("grp", "tp")
    return jax.shard_map(
        body,
        mesh=fine,
        in_specs=(
            P(rows, heads),
            P(rows, heads),
            P(rows, None, heads),
            P(rows, None, heads),
            P(),
            P(),
        ),
        out_specs=(P(rows, heads), P(rows, None, heads), P(rows, None, heads)),
        check_vma=False,
    )
```
